512 devices in a mesh: section: 32 (over y_lo, z), tensor: 16 (over y_hi, x, core).
Axes of the slice: x: 4, y: 4 (y_hi: 2, y_lo: 2; y = y_hi * 2 + y_lo), z: 16, core: 2. Of those that a mesh axis runs over, the one named last changes fastest.
Arguments:
- weight: bfloat16 [32, 2, 2560, 4096], P('section', None, None, 'tensor'), as said below
- stash_in: bfloat16 [32, 2, 2, 128, 2560], P('section', None, None, 'tensor'), may hold values from -6 to 6
- stash_pre: bfloat16 [32, 2, 2, 128, 4096], P('section', None, None, None, 'tensor'), may hold values from -6 to 6
- grad_in: bfloat16 [32, 2, 128, 2560], P('section', None, 'tensor'), may hold values from -1.5 to 1.5
- grad_loss: bfloat16 [2, 128, 2560], P(None, 'tensor'), may hold values from -1.5 to 1.5
Outputs:
- weight_grad: bfloat16 [32, 2560, 4096], P('section', None, 'tensor')
- grad_out: bfloat16 [32, 2, 128, 2560], P('section', None, 'tensor')
The draws below stay inside these ranges and needn't reach their ends.
Inputs may be any that keep to these rules, and one draw needn't show every extreme that they name: weight[s, 1] equals weight[31 - s, 0] for every s: both copies of a section agree.
All inputs are finite; a program needn't handle non-finite values.
Results may differ from the reference program's by a relative error of at most 0.023.
Values may be sent and summed in bfloat16 or wider, within the bound.
No kernel may reach another device: no remote copies, remote signals or barrier semaphores. Data moves between devices by JAX's collectives and lax.ppermute only.
A program may use at most 64 MiB of HBM per device.

```python
import jax
import jax.numpy as jnp
from jax import lax

D = 2560
FF_DEV = 256
SECTIONS = 32
FF = 4096
TOK = 128
N_TENSOR = 16


def draw_weight(key, part):
    key = jax.random.fold_in(key, 7)
    base = (jax.random.normal(key, (SECTIONS, D, FF), jnp.float32) * D ** (-0.5)).astype(jnp.bfloat16)
    return jnp.stack([base, jnp.flip(base, 0)], axis=1)


def level_of(rng, dims, pieces, smallest, high):
    def one(dim, blocks):
        draws = jax.random.uniform(jax.random.fold_in(jax.random.fold_in(rng, 6), dim), (blocks,), jnp.float32, smallest / len(pieces), high / len(pieces))
        return jnp.repeat(jnp.exp(draws), dims[dim] // blocks).reshape((-1,) + (1,) * (len(dims) - dim - 1))

    loudness = one(*pieces[0])
    for cut in pieces[1:]:
        loudness = loudness * one(*cut)
    return loudness


def scatter_about(own_key, extent, width, bound, pieces=(), held_as=jnp.bfloat16):
    result = jax.random.normal(own_key, extent, jnp.float32) * width
    if len(pieces) > 0:
        result = level_of(own_key, extent, pieces, -0.22, 0.18) * result
    return jnp.clip(result, min=-bound, max=bound).astype(held_as)


def setup_inputs(seed: int = 0) -> dict:
    splits = jax.random.split(jax.random.key(seed), 6)
    return {
        "weight": draw_weight(jax.random.fold_in(splits[5], 71), 0),
        "stash_in": scatter_about(splits[1], (SECTIONS, 2, 2, TOK, D), 1.0, 6.0, ((0, 32), (3, 16))),
        "stash_pre": scatter_about(splits[2], (SECTIONS, 2, 2, TOK, FF), 1.0, 6.0, ((0, 32), (4, 16))),
        "grad_in": scatter_about(splits[3], (SECTIONS, 2, TOK, D), 0.25, 1.5, ((0, 32), (2, 16))),
        "grad_loss": scatter_about(splits[4], (2, TOK, D), 0.25, 1.5, ((1, 16),)),
    }


slope_c = 0.7978845608028654
cubic_c = 0.044715


def gelu_value(pre):
    inner = slope_c * (pre + cubic_c * pre * pre * pre)
    return 0.5 * pre * (1.0 + jnp.tanh(inner))


def gelu_slope(pre):
    inner = slope_c * (pre + cubic_c * pre * pre * pre)
    tanh_v = jnp.tanh(inner)
    return 0.5 * (1.0 + tanh_v) + 0.5 * pre * (1.0 - tanh_v * tanh_v) * slope_c * (1.0 + 3.0 * cubic_c * pre * pre)


def settle(value):
    return lax.optimization_barrier(value.astype(jnp.bfloat16)).astype(jnp.float32)


def section_back(weight_k, inputs, pre, cotan):
    pre32 = pre.astype(jnp.float32)
    dhid = jnp.dot(cotan, weight_k, preferred_element_type=jnp.float32)
    dpre = (dhid * gelu_slope(pre32)).astype(jnp.bfloat16)
    hidden = gelu_value(pre32).astype(jnp.bfloat16)
    blocks = dpre.astype(jnp.float32).reshape(TOK, N_TENSOR, FF_DEV)
    wblocks = weight_k.astype(jnp.float32).reshape(D, N_TENSOR, FF_DEV)
    parts = jnp.einsum("tcf,dcf->ctd", blocks, wblocks)
    dx = (jnp.sum(settle(parts), axis=0) + cotan.astype(jnp.float32)).astype(jnp.bfloat16)
    wgrad = jnp.dot(inputs.T, dpre, preferred_element_type=jnp.float32)
    wgrad = wgrad + jnp.dot(cotan.T, hidden, preferred_element_type=jnp.float32)
    return dx, wgrad


def reference(weight, stash_in, stash_pre, grad_in, grad_loss):
    last = SECTIONS - 1
    places = jnp.arange(SECTIONS, dtype=jnp.int32)

    def first(place):
        down = section_back(weight[place, 0], stash_in[place, 0, 0], stash_pre[place, 0, 0], grad_in[place, 0])[0]
        upper = section_back(weight[place, 1], stash_in[place, 1, 0], stash_pre[place, 1, 0], grad_in[place, 1])[0]
        return jnp.stack([down, upper])

    first_dx = lax.map(first, places)
    down_next = jnp.concatenate([first_dx[1:, 0], grad_loss[0][None]], axis=0)
    up_next = jnp.concatenate([grad_loss[1][None], first_dx[:-1, 1]], axis=0)

    def second(section_k):
        mirror = last - section_k
        weight_a = weight[section_k, 0]
        weight_b = weight[mirror, 1]
        unused_a, grad_a1 = section_back(weight_a, stash_in[section_k, 0, 0], stash_pre[section_k, 0, 0], grad_in[section_k, 0])
        down_dx, grad_a2 = section_back(weight_a, stash_in[section_k, 0, 1], stash_pre[section_k, 0, 1], down_next[section_k])
        unused_b, grad_b1 = section_back(weight_b, stash_in[mirror, 1, 0], stash_pre[mirror, 1, 0], grad_in[mirror, 1])
        up_dx, grad_b2 = section_back(weight_b, stash_in[mirror, 1, 1], stash_pre[mirror, 1, 1], up_next[mirror])
        total = (settle(grad_a1 + grad_a2) + settle(grad_b1 + grad_b2)).astype(jnp.bfloat16)
        return total, down_dx, up_dx

    weight_grad, down_out, up_out = lax.map(second, places)
    grad_out = jnp.stack([down_out, jnp.flip(up_out, 0)], axis=1)
    return weight_grad, grad_out
```

```python
import jax
import jax.numpy as jnp
from jax import lax
from jax.sharding import PartitionSpec as P

slope_c = 0.7978845608028654
cubic_c = 0.044715


def gelu_both(pre):
    inner = slope_c * (pre + cubic_c * pre * pre * pre)
    tanh_v = jnp.tanh(inner)
    value = 0.5 * pre * (1.0 + tanh_v)
    slope = 0.5 * (1.0 + tanh_v) + 0.5 * pre * (1.0 - tanh_v * tanh_v) * slope_c * (
        1.0 + 3.0 * cubic_c * pre * pre
    )
    return value, slope


def dot(a, b, over):
    return lax.dot_general(a, b, ((over[:1], over[1:]), ((), ())), preferred_element_type=jnp.float32)


def body(weight, stash_in, stash_pre, grad_in, grad_loss):
    sections = lax.axis_size("section")
    tensors = lax.axis_size("tensor")
    place = lax.axis_index("section")
    core = lax.axis_index("tensor") % 2
    bf16 = jnp.bfloat16
    mirror = [(s, sections - 1 - s) for s in range(sections)]
    swap = [(t, t ^ 1) for t in range(tensors)]
    pairs = ("section", "tensor")

    def flat(s, t):
        return s * tensors + t

    g_far = lax.ppermute(grad_in[0, 1], "section", mirror)
    own_w = weight[0, 0]
    other_w = lax.ppermute(own_w, "tensor", swap)
    pre_a = lax.ppermute(
        stash_pre[0, 1], pairs,
        [(flat(s, t), flat(sections - 1 - s, t)) for s in range(sections) for t in range(1, tensors, 2)],
    )
    pre_b = lax.ppermute(
        jnp.where(core == 0, stash_pre[0, 1], stash_pre[0, 0]), pairs,
        [(flat(s, t), flat(sections - 1 - s, t + 1)) for s in range(sections) for t in range(0, tensors, 2)]
        + [(flat(s, t), flat(s, t - 1)) for s in range(sections) for t in range(1, tensors, 2)],
    )
    x_far = lax.ppermute(stash_in[0, 1], "section", mirror)
    pre_own = jnp.where(core == 0, stash_pre[0, 0], pre_a)

    def to_cores(rows):
        blocks = jnp.broadcast_to(rows[None], (tensors // 2,) + rows.shape)
        blocks = blocks.reshape((tensors,) + rows.shape[1:])
        return lax.all_to_all(blocks, "tensor", 0, 0, tiled=True)

    def sum_rows(part):
        n = part.shape[0] // tensors
        blocks = lax.all_to_all(part.reshape(tensors, n, -1), "tensor", 0, 0, tiled=True)
        blocks = blocks.reshape(tensors // 2, 2, n, -1).astype(jnp.float32)
        return jnp.sum(blocks, axis=0)

    g_rows = jnp.stack([grad_in[0, 0], g_far])
    x_rows = jnp.stack([stash_in[0, 0], x_far])
    cots, dzs, hids = [], [], []
    dx_rows = None
    for tick in range(2):
        cot = to_cores(g_rows)
        cot = cot.reshape(-1, cot.shape[-1])
        h_a, slope_a = gelu_both(pre_own[tick].astype(jnp.float32))
        h_b, slope_b = gelu_both(pre_b[tick].astype(jnp.float32))
        dz_a = (dot(cot, own_w, (1, 0)) * slope_a).astype(bf16)
        dz_b = (dot(cot, other_w, (1, 0)) * slope_b).astype(bf16)
        part = dot(dz_a, own_w, (1, 1)) + dot(dz_b, other_w, (1, 1))
        dx_rows = (sum_rows(part.astype(bf16)) + g_rows.astype(jnp.float32)).astype(bf16)
        cots.append(cot)
        dzs.append((dz_a, dz_b))
        hids.append((h_a.astype(bf16), h_b.astype(bf16)))
        if tick == 0:
            down = lax.ppermute(dx_rows, "section", [(s, s - 1) for s in range(1, sections)])
            g_rows = jnp.where(place == sections - 1, grad_loss, down)
    back = lax.ppermute(dx_rows[1], "section", mirror)
    grad_out = jnp.stack([dx_rows[0], back])[None]

    x_all = to_cores(x_rows)
    x_all = x_all.reshape(-1, x_all.shape[-1])

    def as_x(first, second):
        return jnp.stack([v.reshape(tensors, -1, v.shape[-1]) for v in (first, second)], 1).reshape(
            -1, first.shape[-1]
        )

    left = jnp.concatenate([x_all] + cots, axis=0)
    accs = []
    for side in range(2):
        right = jnp.concatenate(
            [as_x(dzs[0][side], dzs[1][side]), hids[0][side], hids[1][side]], axis=0
        )
        accs.append(dot(left, right, (0, 0)).astype(bf16))
    theirs = lax.ppermute(accs[1], "tensor", swap)
    total = (accs[0].astype(jnp.float32) + theirs.astype(jnp.float32)).astype(bf16)
    return total[None], grad_out


def solution(mesh):
    return jax.shard_map(
        body,
        mesh=mesh,
        in_specs=(
            P("section", None, None, "tensor"),
            P("section", None, None, "tensor", None),
            P("section", None, None, None, "tensor"),
            P("section", None, "tensor", None),
            P(None, "tensor", None),
        ),
        out_specs=(P("section", None, "tensor"), P("section", None, "tensor", None)),
        check_vma=False,
    )
```

```python
import functools

import jax
import jax.numpy as jnp
from jax import lax
from jax.experimental import pallas as pl
from jax.experimental.pallas import tpu as pltpu
from jax.sharding import PartitionSpec as P

slope_c = 0.7978845608028654
cubic_c = 0.044715
bf16, f32 = jnp.bfloat16, jnp.float32
vmem = pltpu.CompilerParams(vmem_limit_bytes=48 * 2**20)


def gelu_both(pre):
    inner = slope_c * (pre + cubic_c * pre * pre * pre)
    tanh_v = jnp.tanh(inner)
    slope = 0.5 * (1.0 + tanh_v) + 0.5 * pre * (1.0 - tanh_v * tanh_v) * slope_c * (
        1.0 + 3.0 * cubic_c * pre * pre
    )
    return 0.5 * pre * (1.0 + tanh_v), slope


def dot(a, b, over):
    return lax.dot_general(a, b, ((over[:1], over[1:]), ((), ())), preferred_element_type=f32)


def of_kind(value, rows, kind):
    split = value.reshape(-1, 2, rows // 2, value.shape[-1])
    return split[:, kind].reshape(-1, value.shape[-1])


def merged(value):
    return value.reshape(-1, value.shape[-1])


def tick_kernel(last, where_ref, cot_ref, w_own, w_other, pre_own, pre_other, extra_ref, out_ref):
    depth = w_own.shape[1]
    tokens = pre_own.shape[2]
    chips, rows = cot_ref.shape[0], cot_ref.shape[-2]
    cot = merged(cot_ref[:, 0]) if last else merged(cot_ref[...])
    dz = []
    for w, pre in ((w_own, pre_own), (w_other, pre_other)):
        slope = gelu_both(pre[0, 0].astype(f32))[1]
        dh = dot(cot, w[0], (1, 0))
        dz.append(((dh if last else of_kind(dh, rows, 0)) * slope).astype(bf16))
    step = 512
    for start in range(0, depth, step):
        at = pl.ds(start, step)
        part = dot(dz[0], w_own[0, at, :], (1, 1)) + dot(dz[1], w_other[0, at, :], (1, 1))
        if last:
            chip = lax.broadcasted_iota(jnp.int32, part.shape, 0) // rows
            part = part + jnp.where(chip == where_ref[1], merged(cot_ref[:, 0, :, at]).astype(f32), 0.0)
            out_ref[:, at] = part.astype(bf16)
        else:
            out_ref[:, 0, :, at] = part.astype(bf16).reshape(out_ref.shape[0], -1, step)
    if not last:
        for chip in range(out_ref.shape[0]):
            out_ref[chip, 1] = extra_ref[...]


def tick_call(tick, where, cot, own_w, other_w, own_pre, other_pre, extra):
    depth, width = own_w.shape[1:]
    tokens, rows = own_pre.shape[2], extra.shape[0]
    last = tick == 1
    w_spec = pl.BlockSpec((1, depth, width), lambda i, at: (at[0], 0, 0))
    pre_spec = pl.BlockSpec((1, 1, tokens, width), lambda i, at: (at[0], tick, 0, 0))
    cot_shape = cot.shape[:1] + (1,) + cot.shape[2:] if last else cot.shape
    shape = (tokens, depth) if last else (tokens // rows, 2, rows, depth)
    return pl.pallas_call(
        functools.partial(tick_kernel, last),
        out_shape=jax.ShapeDtypeStruct(shape, bf16),
        grid_spec=pltpu.PrefetchScalarGridSpec(
            num_scalar_prefetch=1,
            grid=(1,),
            in_specs=[
                pl.BlockSpec(cot_shape, lambda i, at: (0,) * len(cot_shape)),
                w_spec, w_spec, pre_spec, pre_spec,
                pl.BlockSpec((rows, depth), lambda i, at: (0, 0)),
            ],
            out_specs=pl.BlockSpec(shape, lambda i, at: (0,) * len(shape)),
        ),
        compiler_params=vmem,
        cost_estimate=pl.CostEstimate(
            flops=8 * tokens * depth * width, bytes_accessed=10 * depth * width, transcendentals=2 * tokens * width
        ),
    )(where, cot, own_w, other_w, own_pre, other_pre, extra)


def grad_kernel(
    where_ref, one_ref, mid_ref, two_ref, swap_a, swap_b, w_own, w_other, pre_own, pre_other, pre_far, own_ref, other_ref
):
    first = where_ref[0] == 0
    depth = own_ref.shape[0]
    width = own_ref.shape[1]
    tokens, rows = swap_a.shape[0], one_ref.shape[-2]

    def left_one(at):
        return jnp.where(first, merged(one_ref[:, :, at]), jnp.concatenate([merged(mid_ref[:, 1, :, at]), swap_a[:, at]]))

    cot_one = left_one(slice(None))
    cot_two = jnp.where(first, merged(two_ref[:, 0]), merged(two_ref[:, 1]))
    rights = []
    for side, (w, pre) in enumerate(((w_own, pre_own), (w_other, pre_other))):
        (hid_one, slope_one), (hid_two, slope_two) = (
            gelu_both(jnp.where(first, pre[0, tick], pre_far[side, tick]).astype(f32)) for tick in range(2)
        )
        dh = dot(cot_one, w[0], (1, 0))
        dz_one = jnp.where(first, of_kind(dh, rows, 0), dh[:tokens]) * slope_one
        dz_two = dot(cot_two, w[0], (1, 0)) * slope_two
        in_turn = jnp.stack([value.reshape(-1, rows // 2, width) for value in (hid_one, dz_one)], 1)
        pair = jnp.where(first, in_turn.reshape(-1, width), jnp.concatenate([hid_one, dz_one]))
        rights.append(jnp.concatenate([pair.astype(bf16), dz_two.astype(bf16), hid_two.astype(bf16)]))
    right = jnp.concatenate(rights, axis=1)
    step = 256
    for start in range(0, depth, step):
        at = pl.ds(start, step)
        left = [
            cot_one[:, start : start + step],
            jnp.where(first, swap_a[:, at], swap_b[:, at]),
            cot_two[:, start : start + step],
        ]
        acc = dot(jnp.concatenate(left, axis=0), right, (0, 0)).astype(bf16)
        own_ref[at, :] = acc[:, :width]
        other_ref[at, :] = acc[:, width:]


def grad_call(where, one, mid, two, swap_a, swap_b, own_w, other_w, own_pre, other_pre, far_pre):
    depth, width = own_w.shape[1:]

    def whole(value, shape=None):
        return pl.BlockSpec(shape or value.shape, lambda i, at: (0,) * value.ndim)

    w_shape, pre_shape = (1,) + own_w.shape[1:], (1,) + own_pre.shape[1:]
    out = jax.ShapeDtypeStruct((depth, width), bf16)
    return pl.pallas_call(
        grad_kernel,
        out_shape=(out, out),
        grid_spec=pltpu.PrefetchScalarGridSpec(
            num_scalar_prefetch=1,
            grid=(1,),
            in_specs=[
                whole(one), whole(mid), whole(two), whole(swap_a), whole(swap_b),
                whole(own_w, w_shape), whole(other_w, w_shape),
                whole(own_pre, pre_shape), whole(other_pre, pre_shape), whole(far_pre),
            ],
            out_specs=(whole(out), whole(out)),
        ),
        compiler_params=vmem,
        cost_estimate=pl.CostEstimate(
            flops=12 * 256 * depth * width, bytes_accessed=16 * depth * width, transcendentals=1 << 17
        ),
    )(where, one, mid, two, swap_a, swap_b, own_w, other_w, own_pre, other_pre, far_pre)


def body(weight, stash_in, stash_pre, grad_in, grad_loss):
    sections = lax.axis_size("section")
    tensors = lax.axis_size("tensor")
    chips = tensors // 2
    end = sections - 1
    place = lax.axis_index("section")
    chip = lax.axis_index("tensor") // 2
    core = lax.axis_index("tensor") % 2
    where = jnp.stack([core, chip]).astype(jnp.int32)
    swap = [(t, t ^ 1) for t in range(tensors)]
    same_core = [[2 * j + c for j in range(chips)] for c in range(2)]
    pairs = ("section", "tensor")

    def pick(zero, one):
        return jnp.where(core == 0, zero, one)

    def moves(zero, one, flip=0):
        out = []
        for t in range(tensors):
            out += [(a * tensors + t, b * tensors + (t ^ flip)) for a, b in (one if t % 2 else zero)]
        return out

    def exchange(blocks):
        return lax.all_to_all(blocks, "tensor", 0, 0, tiled=True, axis_index_groups=same_core)

    def to_chips(rows):
        return jnp.broadcast_to(rows[None], (chips,) + rows.shape)

    def both_cores(kept, came):
        return pick(jnp.concatenate([kept, came], -2), jnp.concatenate([came, kept], -2))

    mirror = [(s, end - s) for s in range(sections)]
    down = [(s, s - 1) for s in range(1, sections)]
    up = [(s, s + 1) for s in range(end)]
    home_up = [(s, end - (s + 1)) for s in range(end)]

    own_w, own_pre = weight[0], stash_pre[0]
    x, g = stash_in[0], grad_in[0]

    n, depth = g.shape[1:]

    for_cores = jnp.stack([jnp.concatenate([g[p], x[0, p]]) for p in range(2)])
    one = lax.all_to_all(
        jnp.broadcast_to(for_cores[None], (chips,) + for_cores.shape).reshape(tensors, 2 * n, depth),
        "tensor", 0, 0, tiled=True,
    )
    other_w = lax.ppermute(own_w, "tensor", swap)
    other_pre = lax.ppermute(own_pre, "tensor", swap)

    far_g = jnp.stack([g[1], g[1]])
    far_a = lax.ppermute(pick(x[1], far_g), pairs, moves(mirror, mirror))
    far_b = lax.ppermute(pick(far_g, x[1]), pairs, moves(mirror, mirror, 1))
    far = both_cores(far_a, far_b)
    far_pre = lax.ppermute(jnp.stack([own_pre[1], other_pre[1]]), pairs, moves([], mirror))
    loss = both_cores(
        pick(grad_loss[0], grad_loss[1]), lax.ppermute(pick(grad_loss[1], grad_loss[0]), "tensor", swap)
    )

    part = tick_call(0, where, one, own_w, other_w, own_pre, other_pre, far[0])
    mid = exchange(part)
    mid, far_pre, loss = lax.optimization_barrier((mid, far_pre, loss))

    mine = lax.dynamic_slice_in_dim(one, 2 * chip, 2, 0)[:, :n].reshape(2 * n, depth)
    dx = (jnp.sum(mid[:, 0].astype(f32), axis=0) + mine.astype(f32)).astype(bf16)
    next_g = lax.ppermute(dx, pairs, moves(down, up))
    next_far = lax.ppermute(dx, pairs, moves([], home_up))
    next_g = jnp.where(place == pick(end, 0), loss, next_g)
    next_far = pick(far[1], jnp.where(place == end, loss, next_far))
    two = exchange(to_chips(jnp.stack([next_g, next_far])))
    swap_a = lax.ppermute(merged(pick(mid[:, 1], one[:, n:].reshape(mid[:, 1].shape))), "tensor", swap)
    two, swap_a = lax.optimization_barrier((two, swap_a))

    part = tick_call(1, where, two, own_w, other_w, own_pre, other_pre, far[1])
    part, late = lax.optimization_barrier((part, two))
    blocks = lax.all_to_all(part.reshape(tensors, n, depth), "tensor", 0, 0, tiled=True)
    swap_b = lax.ppermute(merged(late[:, 1]), "tensor", [(t, t + 1) for t in range(0, tensors, 2)])
    own, other = grad_call(where, one, mid, late, swap_a, swap_b, own_w, other_w, own_pre, other_pre, far_pre)
    blocks, own, other = lax.optimization_barrier((blocks, own, other))
    theirs = lax.ppermute(other, "tensor", swap)
    grad_out = jnp.sum(blocks.reshape(chips, 2, n, depth).astype(f32), axis=0).astype(bf16)[None]
    total = (own.astype(f32) + theirs.astype(f32)).astype(bf16)
    return total[None], grad_out


def solution(mesh):
    return jax.shard_map(
        body,
        mesh=mesh,
        in_specs=(
            P("section", None, None, "tensor"),
            P("section", None, None, "tensor", None),
            P("section", None, None, None, "tensor"),
            P("section", None, "tensor", None),
            P(None, "tensor", None),
        ),
        out_specs=(P("section", None, "tensor"), P("section", None, "tensor", None)),
        check_vma=False,
    )
```

```python
import functools

import jax
import jax.numpy as jnp
from jax import lax
from jax.experimental import pallas as pl
from jax.experimental.pallas import tpu as pltpu
from jax.sharding import PartitionSpec as P

slope_c = 0.7978845608028654
cubic_c = 0.044715
bf16, f32 = jnp.bfloat16, jnp.float32
vmem = pltpu.CompilerParams(vmem_limit_bytes=48 * 2**20)


def gelu_both(pre):
    inner = slope_c * (pre + cubic_c * pre * pre * pre)
    tanh_v = jnp.tanh(inner)
    slope = 0.5 * (1.0 + tanh_v) + 0.5 * pre * (1.0 - tanh_v * tanh_v) * slope_c * (
        1.0 + 3.0 * cubic_c * pre * pre
    )
    return 0.5 * pre * (1.0 + tanh_v), slope


def dot(a, b, over):
    return lax.dot_general(a, b, ((over[:1], over[1:]), ((), ())), preferred_element_type=f32)


def of_kind(value, rows, kind):
    split = value.reshape(-1, 2, rows // 2, value.shape[-1])
    return split[:, kind].reshape(-1, value.shape[-1])


def merged(value):
    return value.reshape(-1, value.shape[-1])


def tick_kernel(last, where_ref, cot_ref, w_own, w_other, pre_own, pre_other, out_ref):
    chips, rows, depth = out_ref.shape
    turn = cot_ref.shape[-2]
    cot = merged(cot_ref[:, 0]) if last else merged(cot_ref[...])
    dz = []
    for w, pre in ((w_own, pre_own), (w_other, pre_other)):
        slope = gelu_both(pre[0, 0].astype(f32))[1]
        dh = dot(cot, w[0], (1, 0))
        dz.append(((dh if last else of_kind(dh, turn, 0)) * slope).astype(bf16))
    step = 512
    for start in range(0, depth, step):
        at = pl.ds(start, step)
        part = dot(dz[0], w_own[0, at, :], (1, 1)) + dot(dz[1], w_other[0, at, :], (1, 1))
        chip = lax.broadcasted_iota(jnp.int32, part.shape, 0) // rows
        added = cot[:, start : start + step].astype(f32)
        part = part + jnp.where(chip == where_ref[1], added if last else of_kind(added, turn, 0), 0.0)
        out_ref[:, :, at] = part.astype(bf16).reshape(chips, rows, step)


def tick_call(tick, where, cot, own_w, other_w, own_pre, other_pre):
    depth, width = own_w.shape[1:]
    tokens = own_pre.shape[2]
    rows = 16
    w_specs = [pl.BlockSpec((1, depth, width), lambda i, at, own=own: (at[0] * own, 0, 0)) for own in (1, 0)]
    pre_specs = [pl.BlockSpec((1, 1, tokens, width), lambda i, at, own=own: (at[0] * own, tick, 0, 0)) for own in (1, 0)]
    cot_shape = cot.shape[:1] + (1,) + cot.shape[2:] if tick == 1 else cot.shape
    shape = (tokens // rows, rows, depth)
    return pl.pallas_call(
        functools.partial(tick_kernel, tick == 1),
        out_shape=pltpu.HBM(shape, bf16),
        grid_spec=pltpu.PrefetchScalarGridSpec(
            num_scalar_prefetch=1,
            grid=(1,),
            in_specs=[
                pl.BlockSpec(cot_shape, lambda i, at: (0,) * len(cot_shape)),
                *w_specs, *pre_specs,
            ],
            out_specs=pl.BlockSpec(shape, lambda i, at: (0,) * len(shape)),
        ),
        compiler_params=vmem,
        cost_estimate=pl.CostEstimate(
            flops=8 * tokens * depth * width, bytes_accessed=10 * depth * width, transcendentals=2 * tokens * width
        ),
    )(where, cot, own_w, other_w, own_pre, other_pre)


def grad_kernel(where_ref, one_ref, one_came, two_ref, two_came, w_ref, pre_near, pre_far, out_ref):
    depth, width = out_ref.shape
    tokens, turn = pre_near.shape[2], one_ref.shape[-2]

    def in_turn(kinds):
        return jnp.stack([kind.reshape(-1, turn // 2, width) for kind in kinds], 1).reshape(-1, width).astype(bf16)

    def form(one_a, one_b, two_a, two_b):
        w = w_ref[0]
        (hid_1, slope_1), (hid_2, slope_2) = (gelu_both(pre_near[0, tick].astype(f32)) for tick in range(2))
        dz_1 = of_kind(dot(merged(one_a[...]), w, (1, 0)), turn, 0) * slope_1
        dz_2 = dot(merged(two_a[:, 0]), w, (1, 0)) * slope_2
        right_near = jnp.concatenate([in_turn((hid_1, dz_1)), in_turn((jnp.zeros_like(dz_2), dz_2)), hid_2.astype(bf16)])
        rights = []
        for tick in range(2):
            hid, slope = gelu_both(pre_far[0, tick].astype(f32))
            dz = dot(merged(two_b[:, 1 + tick]), w, (1, 0)) * slope
            rights += [dz.astype(bf16), hid.astype(bf16)]
        right_far = jnp.concatenate(rights)
        step = 256
        for start in range(0, depth, step):
            at = pl.ds(start, step)
            left = jnp.concatenate([merged(one_a[:, :, at]), merged(one_b[:, :, at]), merged(two_a[:, 0, :, at])])
            near = dot(left, right_near, (0, 0)).astype(bf16)
            left = jnp.concatenate(
                [merged(ref[:, 1 + tick, :, at]) for tick in range(2) for ref in (two_a, two_b)]
            )
            far = dot(left, right_far, (0, 0)).astype(bf16)
            out_ref[at, :] = (near.astype(f32) + far.astype(f32)).astype(bf16)

    @pl.when(where_ref[0] == 0)
    def _():
        form(one_ref, one_came, two_ref, two_came)

    @pl.when(where_ref[0] == 1)
    def _():
        form(one_came, one_ref, two_came, two_ref)


def grad_call(where, one, one_came, two, two_came, own_w, own_pre, far_pre):
    depth, width = own_w.shape[1:]

    def whole(value, shape=None):
        return pl.BlockSpec(shape or value.shape, lambda i, at: (0,) * value.ndim)

    out = jax.ShapeDtypeStruct((depth, width), bf16)
    return pl.pallas_call(
        grad_kernel,
        out_shape=out,
        grid_spec=pltpu.PrefetchScalarGridSpec(
            num_scalar_prefetch=1,
            grid=(1,),
            in_specs=[
                whole(one), whole(one_came), whole(two), whole(two_came), whole(own_w, (1,) + own_w.shape[1:]),
                whole(own_pre, (1,) + own_pre.shape[1:]), whole(far_pre),
            ],
            out_specs=whole(out),
        ),
        compiler_params=vmem,
        cost_estimate=pl.CostEstimate(
            flops=12 * 256 * depth * width, bytes_accessed=16 * depth * width, transcendentals=1 << 17
        ),
    )(where, one, one_came, two, two_came, own_w, own_pre, far_pre)


def body(weight, stash_in, stash_pre, grad_in, grad_loss):
    sections = lax.axis_size("section")
    tensors = lax.axis_size("tensor")
    chips = tensors // 2
    end = sections - 1
    place = lax.axis_index("section")
    chip = lax.axis_index("tensor") // 2
    core = lax.axis_index("tensor") % 2
    where = jnp.stack([core, chip]).astype(jnp.int32)
    swap = [(t, t ^ 1) for t in range(tensors)]
    same_core = [[2 * j + c for j in range(chips)] for c in range(2)]
    pairs = ("section", "tensor")

    def pick(zero, one):
        return jnp.where(core == 0, zero, one)

    def moves(zero, one, flip=0):
        out = []
        for t in range(tensors):
            out += [(a * tensors + t, b * tensors + (t ^ flip)) for a, b in (one if t % 2 else zero)]
        return out

    def exchange(blocks):
        return lax.all_to_all(blocks, "tensor", 0, 0, tiled=True, axis_index_groups=same_core)

    def to_chips(rows):
        return jnp.broadcast_to(rows[None], (chips,) + rows.shape)

    def both_cores(kept, came):
        return pick(jnp.concatenate([kept, came], -2), jnp.concatenate([came, kept], -2))

    mirror = [(s, end - s) for s in range(sections)]
    down = [(s, s - 1) for s in range(1, sections)]
    up = [(s, s + 1) for s in range(end)]
    home_up = [(s, end - (s + 1)) for s in range(end)]

    own_w, own_pre = weight[0], stash_pre[0]
    x, g = stash_in[0], grad_in[0]

    n, depth = g.shape[1:]

    for_cores = jnp.stack([jnp.concatenate([g[p], x[0, p]]) for p in range(2)])
    one = lax.all_to_all(
        jnp.broadcast_to(for_cores[None], (chips,) + for_cores.shape).reshape(tensors, 2 * n, depth),
        "tensor", 0, 0, tiled=True,
    )
    other_w = lax.ppermute(pick(own_w[1:], own_w[:1]), "tensor", swap)
    other_pre = lax.ppermute(pick(own_pre[1:], own_pre[:1]), "tensor", swap)

    far_g = jnp.stack([g[1], g[1]])
    far_a = lax.ppermute(pick(x[1], far_g), pairs, moves(mirror, mirror))
    far_b = lax.ppermute(pick(far_g, x[1]), pairs, moves(mirror, mirror, 1))
    far = both_cores(far_a, far_b)
    far_pre = lax.ppermute(own_pre[1:], "section", mirror)

    part = tick_call(0, where, one, own_w, other_w, own_pre, other_pre)
    mid = exchange(part)
    mid, far = lax.optimization_barrier((mid, far))

    begin = place == pick(end, 0)
    last_sends = place == pick(0, end)
    dx = jnp.sum(mid.astype(f32), axis=0).astype(bf16)
    own_loss, for_other = pick(grad_loss[0], grad_loss[1]), pick(grad_loss[1], grad_loss[0])
    doubled = jnp.concatenate([for_other, for_other])
    at_end = [(end * tensors + t, end * tensors + t + 1) for t in range(0, tensors, 2)]
    at_ends = [(t, t + 1) for t in range(0, tensors, 2)] + [(b, a) for a, b in at_end]
    next_far = lax.ppermute(pick(doubled, dx), pairs, moves([], home_up) + at_end)
    next_g = lax.ppermute(jnp.where(last_sends, doubled, dx), pairs, moves(down, up) + at_ends)
    next_g = jnp.where(begin, both_cores(own_loss, next_g[:n]), next_g)
    next_far = pick(far[1], jnp.where(place == end, both_cores(own_loss, next_far[:n]), next_far))
    two = exchange(to_chips(jnp.stack([next_g, far[0], next_far])))
    one_came = lax.ppermute(one, "tensor", swap)
    two, one_came, far_pre = lax.optimization_barrier((two, one_came, far_pre))

    part = tick_call(1, where, two, own_w, other_w, own_pre, other_pre)
    part, late = lax.optimization_barrier((part, two))
    blocks = lax.all_to_all(part.reshape(tensors, n, depth), "tensor", 0, 0, tiled=True)
    two_came = lax.ppermute(late, "tensor", swap)
    total = grad_call(where, one, one_came, late, two_came, own_w, own_pre, far_pre)
    blocks, total = lax.optimization_barrier((blocks, total))
    grad_out = jnp.sum(blocks.reshape(chips, 2, n, depth).astype(f32), axis=0).astype(bf16)[None]
    return total[None], grad_out


def solution(mesh):
    return jax.shard_map(
        body,
        mesh=mesh,
        in_specs=(
            P("section", None, None, "tensor"),
            P("section", None, None, "tensor", None),
            P("section", None, None, None, "tensor"),
            P("section", None, "tensor", None),
            P(None, "tensor", None),
        ),
        out_specs=(P("section", None, "tensor"), P("section", None, "tensor", None)),
        check_vma=False,
    )
```

```python
import functools

import jax
import jax.numpy as jnp
from jax import lax
from jax.experimental import pallas as pl
from jax.experimental.pallas import tpu as pltpu
from jax.sharding import PartitionSpec as P

slope_c = 0.7978845608028654
cubic_c = 0.044715
bf16, f32 = jnp.bfloat16, jnp.float32
vmem = pltpu.CompilerParams(vmem_limit_bytes=48 * 2**20)


def gelu_both(pre):
    inner = slope_c * (pre + cubic_c * pre * pre * pre)
    tanh_v = jnp.tanh(inner)
    slope = 0.5 * (1.0 + tanh_v) + 0.5 * pre * (1.0 - tanh_v * tanh_v) * slope_c * (
        1.0 + 3.0 * cubic_c * pre * pre
    )
    return 0.5 * pre * (1.0 + tanh_v), slope


def dot(a, b, over):
    return lax.dot_general(a, b, ((over[:1], over[1:]), ((), ())), preferred_element_type=f32)


def of_kind(value, rows, kind):
    split = value.reshape(-1, 2, rows // 2, value.shape[-1])
    return split[:, kind].reshape(-1, value.shape[-1])


def merged(value):
    return value.reshape(-1, value.shape[-1])


def tick_kernel(last, where_ref, cot_ref, w_own, *refs):
    *w_halves, pre_own, pre_other, out_ref = refs
    chips, rows, depth = out_ref.shape
    turn = cot_ref.shape[-2]
    half = depth // 2
    cot = merged(cot_ref[:, 0]) if last else merged(cot_ref[...])
    dh_own = dot(cot, w_own[0], (1, 0))
    dh_other = sum(dot(cot[:, k * half : (k + 1) * half], w[0], (1, 0)) for k, w in enumerate(w_halves))
    dz = []
    for dh, pre in ((dh_own, pre_own), (dh_other, pre_other)):
        slope = gelu_both(pre[0, 0].astype(f32))[1]
        dz.append(((dh if last else of_kind(dh, turn, 0)) * slope).astype(bf16))
    step = half // 2
    for start in range(0, depth, step):
        at, inside = pl.ds(start, step), pl.ds(start % half, step)
        part = dot(dz[0], w_own[0, at, :], (1, 1)) + dot(dz[1], w_halves[start // half][0, inside, :], (1, 1))
        chip = lax.broadcasted_iota(jnp.int32, part.shape, 0) // rows
        added = cot[:, start : start + step].astype(f32)
        part = part + jnp.where(chip == where_ref[1], added if last else of_kind(added, turn, 0), 0.0)
        out_ref[:, :, at] = part.astype(bf16).reshape(chips, rows, step)


def tick_call(tick, where, cot, own_w, other_w, own_pre, other_pre):
    depth, width = own_w.shape[1:]
    tokens = own_pre.shape[2]
    rows = 16
    w_specs = [pl.BlockSpec((1, depth, width), lambda i, at: (at[0], 0, 0))]
    w_specs += [pl.BlockSpec(w.shape, lambda i, at: (0, 0, 0)) for w in other_w]
    pre_specs = [pl.BlockSpec((1, 1, tokens, width), lambda i, at, own=own: (at[0] * own, tick, 0, 0)) for own in (1, 0)]
    cot_shape = cot.shape[:1] + (1,) + cot.shape[2:] if tick == 1 else cot.shape
    shape = (tokens // rows, rows, depth)
    return pl.pallas_call(
        functools.partial(tick_kernel, tick == 1),
        out_shape=pltpu.HBM(shape, bf16),
        grid_spec=pltpu.PrefetchScalarGridSpec(
            num_scalar_prefetch=1,
            grid=(1,),
            in_specs=[
                pl.BlockSpec(cot_shape, lambda i, at: (0,) * len(cot_shape)),
                *w_specs, *pre_specs,
            ],
            out_specs=pl.BlockSpec(shape, lambda i, at: (0,) * len(shape)),
        ),
        compiler_params=vmem,
        cost_estimate=pl.CostEstimate(
            flops=8 * tokens * depth * width, bytes_accessed=10 * depth * width, transcendentals=2 * tokens * width
        ),
    )(where, cot, own_w, *other_w, own_pre, other_pre)


def grad_kernel(where_ref, one_ref, one_came, two_ref, two_came, w_ref, pre_near, pre_far, out_ref):
    depth, width = out_ref.shape
    tokens, turn = pre_near.shape[2], one_ref.shape[-2]

    def in_turn(kinds):
        return jnp.stack([kind.reshape(-1, turn // 2, width) for kind in kinds], 1).reshape(-1, width).astype(bf16)

    def form(one_a, one_b, two_a, two_b):
        w = w_ref[0]
        (hid_1, slope_1), (hid_2, slope_2) = (gelu_both(pre_near[0, tick].astype(f32)) for tick in range(2))
        dz_1 = of_kind(dot(merged(one_a[...]), w, (1, 0)), turn, 0) * slope_1
        dz_2 = dot(merged(two_a[:, 0]), w, (1, 0)) * slope_2
        right_near = jnp.concatenate([in_turn((hid_1, dz_1)), in_turn((jnp.zeros_like(dz_2), dz_2)), hid_2.astype(bf16)])
        rights = []
        for tick in range(2):
            hid, slope = gelu_both(pre_far[0, tick].astype(f32))
            dz = dot(merged(two_b[:, 1 + tick]), w, (1, 0)) * slope
            rights += [dz.astype(bf16), hid.astype(bf16)]
        right_far = jnp.concatenate(rights)
        step = 256
        for start in range(0, depth, step):
            at = pl.ds(start, step)
            left = jnp.concatenate([merged(one_a[:, :, at]), merged(one_b[:, :, at]), merged(two_a[:, 0, :, at])])
            near = dot(left, right_near, (0, 0)).astype(bf16)
            left = jnp.concatenate(
                [merged(ref[:, 1 + tick, :, at]) for tick in range(2) for ref in (two_a, two_b)]
            )
            far = dot(left, right_far, (0, 0)).astype(bf16)
            out_ref[at, :] = (near.astype(f32) + far.astype(f32)).astype(bf16)

    @pl.when(where_ref[0] == 0)
    def _():
        form(one_ref, one_came, two_ref, two_came)

    @pl.when(where_ref[0] == 1)
    def _():
        form(one_came, one_ref, two_came, two_ref)


def grad_call(where, one, one_came, two, two_came, own_w, own_pre, far_pre):
    depth, width = own_w.shape[1:]

    def whole(value, shape=None):
        return pl.BlockSpec(shape or value.shape, lambda i, at: (0,) * value.ndim)

    out = jax.ShapeDtypeStruct((depth, width), bf16)
    return pl.pallas_call(
        grad_kernel,
        out_shape=out,
        grid_spec=pltpu.PrefetchScalarGridSpec(
            num_scalar_prefetch=1,
            grid=(1,),
            in_specs=[
                whole(one), whole(one_came), whole(two), whole(two_came), whole(own_w, (1,) + own_w.shape[1:]),
                whole(own_pre, (1,) + own_pre.shape[1:]), whole(far_pre),
            ],
            out_specs=whole(out),
        ),
        compiler_params=vmem,
        cost_estimate=pl.CostEstimate(
            flops=12 * 256 * depth * width, bytes_accessed=16 * depth * width, transcendentals=1 << 17
        ),
    )(where, one, one_came, two, two_came, own_w, own_pre, far_pre)


def body(weight, stash_in, stash_pre, grad_in, grad_loss):
    sections = lax.axis_size("section")
    tensors = lax.axis_size("tensor")
    chips = tensors // 2
    end = sections - 1
    place = lax.axis_index("section")
    chip = lax.axis_index("tensor") // 2
    core = lax.axis_index("tensor") % 2
    where = jnp.stack([core, chip]).astype(jnp.int32)
    swap = [(t, t ^ 1) for t in range(tensors)]
    same_core = [[2 * j + c for j in range(chips)] for c in range(2)]
    pairs = ("section", "tensor")

    def pick(zero, one):
        return jnp.where(core == 0, zero, one)

    def moves(zero, one, flip=0):
        out = []
        for t in range(tensors):
            out += [(a * tensors + t, b * tensors + (t ^ flip)) for a, b in (one if t % 2 else zero)]
        return out

    def exchange(blocks):
        return lax.all_to_all(blocks, "tensor", 0, 0, tiled=True, axis_index_groups=same_core)

    def to_chips(rows):
        return jnp.broadcast_to(rows[None], (chips,) + rows.shape)

    def both_cores(kept, came):
        return pick(jnp.concatenate([kept, came], -2), jnp.concatenate([came, kept], -2))

    mirror = [(s, end - s) for s in range(sections)]
    down = [(s, s - 1) for s in range(1, sections)]
    up = [(s, s + 1) for s in range(end)]
    home_up = [(s, end - (s + 1)) for s in range(end)]

    own_w, own_pre = weight[0], stash_pre[0]
    x, g = stash_in[0], grad_in[0]

    n, depth = g.shape[1:]

    for_cores = jnp.stack([jnp.concatenate([g[p], x[0, p]]) for p in range(2)])
    one = lax.all_to_all(
        jnp.broadcast_to(for_cores[None], (chips,) + for_cores.shape).reshape(tensors, 2 * n, depth),
        "tensor", 0, 0, tiled=True,
    )
    half = depth // 2
    other_w = [
        lax.ppermute(
            lax.dynamic_slice(own_w, (1 - core, k * half, 0), (1, half, own_w.shape[2])), "tensor", swap
        )
        for k in range(2)
    ]
    other_pre = lax.ppermute(pick(own_pre[1:], own_pre[:1]), "tensor", swap)

    far_g = jnp.stack([g[1], g[1]])
    far_a = lax.ppermute(pick(x[1], far_g), pairs, moves(mirror, mirror))
    far_b = lax.ppermute(pick(far_g, x[1]), pairs, moves(mirror, mirror, 1))
    far = both_cores(far_a, far_b)
    far_pre = lax.ppermute(own_pre[1:], "section", mirror)

    part = tick_call(0, where, one, own_w, other_w, own_pre, other_pre)
    mid = exchange(part)
    mid, far = lax.optimization_barrier((mid, far))

    begin = place == pick(end, 0)
    last_sends = place == pick(0, end)
    dx = jnp.sum(mid.astype(f32), axis=0).astype(bf16)
    own_loss, for_other = pick(grad_loss[0], grad_loss[1]), pick(grad_loss[1], grad_loss[0])
    doubled = jnp.concatenate([for_other, for_other])
    at_end = [(end * tensors + t, end * tensors + t + 1) for t in range(0, tensors, 2)]
    at_ends = [(t, t + 1) for t in range(0, tensors, 2)] + [(b, a) for a, b in at_end]
    next_far = lax.ppermute(pick(doubled, dx), pairs, moves([], home_up) + at_end)
    next_g = lax.ppermute(jnp.where(last_sends, doubled, dx), pairs, moves(down, up) + at_ends)
    next_g = jnp.where(begin, both_cores(own_loss, next_g[:n]), next_g)
    next_far = pick(far[1], jnp.where(place == end, both_cores(own_loss, next_far[:n]), next_far))
    two = exchange(to_chips(jnp.stack([next_g, far[0], next_far])))
    one_came = lax.ppermute(one, "tensor", swap)
    two, one_came, far_pre = lax.optimization_barrier((two, one_came, far_pre))

    part = tick_call(1, where, two, own_w, other_w, own_pre, other_pre)
    part, late = lax.optimization_barrier((part, two))
    blocks = lax.all_to_all(part.reshape(tensors, n, depth), "tensor", 0, 0, tiled=True)
    two_came = lax.ppermute(late, "tensor", swap)
    total = grad_call(where, one, one_came, late, two_came, own_w, own_pre, far_pre)
    blocks, total = lax.optimization_barrier((blocks, total))
    grad_out = jnp.sum(blocks.reshape(chips, 2, n, depth).astype(f32), axis=0).astype(bf16)[None]
    return total[None], grad_out


def solution(mesh):
    return jax.shard_map(
        body,
        mesh=mesh,
        in_specs=(
            P("section", None, None, "tensor"),
            P("section", None, None, "tensor", None),
            P("section", None, None, None, "tensor"),
            P("section", None, "tensor", None),
            P(None, "tensor", None),
        ),
        out_specs=(P("section", None, "tensor"), P("section", None, "tensor", None)),
        check_vma=False,
    )
```
